256 devices in a mesh: lat: 8 (over x, y_lo), lon: 32 (over y_hi, z, core).
Axes of the slice: x: 4, y: 4 (y_hi: 2, y_lo: 2; y = y_hi * 2 + y_lo), z: 8, core: 2. Of those that a mesh axis runs over, the one named last changes fastest.
Arguments:
- tokens: bfloat16 [192, 1536, 512], P('lat', 'lon'), may hold values from -6 to 6
- attend_gain: float32 [512], replicated, may hold values from 0.5 to 1.5
- attend_inward: bfloat16 [512, 1536], replicated, may hold values from -0.25 to 0.25
- attend_outward: bfloat16 [512, 512], replicated, may hold values from -0.25 to 0.25
- expand_gain: float32 [512], replicated, may hold values from 0.5 to 1.5
- expand_weight: bfloat16 [512, 2048], replicated, may hold values from -0.25 to 0.25
- reduce_weight: bfloat16 [2048, 512], replicated, may hold values from -0.125 to 0.125
- merge_gain: float32 [2048], replicated, may hold values from 0.5 to 1.5
- merge_weight: bfloat16 [2048, 1024], replicated, may hold values from -0.125 to 0.125
- coarse_gain: float32 [1024], replicated, may hold values from 0.5 to 1.5
- coarse_inward: bfloat16 [1024, 3072], P('lon'), may hold values from -0.1875 to 0.1875
- coarse_outward: bfloat16 [1024, 1024], P('lon'), may hold values from -0.1875 to 0.1875
Outputs:
- coarse_tokens: bfloat16 [96, 768, 1024], P('lat', 'lon')
The draws below stay inside these ranges and needn't reach their ends.
All inputs are finite; a program needn't handle non-finite values.
Results may differ from the reference program's by a relative error of at most 0.02.
Values may be sent and summed in bfloat16 or wider, within the bound.
A program may use at most 128 MiB of HBM per device.

```python
import jax
import jax.numpy as jnp
from jax import lax

C1 = 512
C2 = 1024
HEADS1 = 8
HEADS2 = 16
FF1 = 2048
WIN_R = 6
WIN_C = 12
SHIFT_R = 3
SHIFT_C = 6
NH = 192
NW = 1536


def steps_of(stream_key, dims, pieces, least, top_value):
    level, own = 1.0, jax.random.fold_in(stream_key, 6)
    for position, blocks in pieces:
        draws = jnp.exp(jax.random.uniform(jax.random.fold_in(own, position), (blocks,), jnp.float32, least / len(pieces), top_value / len(pieces)))
        level = level * jnp.repeat(draws, dims[position] // blocks).reshape([-1 if axis == position else 1 for axis in range(len(dims))])
    return level


def scatter_about(stream_key, shape, spread, limit, split=(), held_as=jnp.bfloat16):
    loudness = steps_of(stream_key, shape, split, -0.22, 0.18) if split else 1.0
    entries = jax.random.normal(stream_key, shape, jnp.float32) * spread * loudness
    return jnp.minimum(jnp.maximum(entries, -limit), limit).astype(held_as)


def setup_inputs(seed: int = 0) -> dict:
    key_of = jax.random.split(jax.random.key(seed), 13)
    return {
        "tokens": scatter_about(key_of[0], (NH, NW, C1), 1.0, 6.0, ((0, 8), (1, 32))),
        "attend_gain": jnp.clip(jax.random.uniform(key_of[1], (C1,), jnp.float32, 0.5, 1.5), 0.5, 1.5),
        "attend_inward": scatter_about(key_of[2], (C1, 3 * C1), C1 ** -0.5, 0.25),
        "attend_outward": scatter_about(key_of[3], (C1, C1), C1 ** -0.5, 0.25),
        "expand_gain": jnp.clip(jax.random.uniform(key_of[4], (C1,), jnp.float32, 0.5, 1.5), 0.5, 1.5),
        "expand_weight": scatter_about(key_of[5], (C1, FF1), C1 ** -0.5, 0.25),
        "reduce_weight": scatter_about(key_of[6], (FF1, C1), FF1 ** -0.5, 0.125),
        "merge_gain": jnp.clip(jax.random.uniform(key_of[7], (4 * C1,), jnp.float32, 0.5, 1.5), 0.5, 1.5),
        "merge_weight": scatter_about(key_of[8], (4 * C1, C2), (4 * C1) ** -0.5, 0.125),
        "coarse_gain": jnp.clip(jax.random.uniform(key_of[9], (C2,), jnp.float32, 0.5, 1.5), 0.5, 1.5),
        "coarse_inward": scatter_about(key_of[10], (C2, 3 * C2), C2 ** -0.5, 0.1875, ((0, 32),)),
        "coarse_outward": scatter_about(key_of[11], (C2, C2), C2 ** -0.5, 0.1875, ((0, 32),)),
    }


NORM_EPS = 1e-05

def layer_norm(values, norm_gain):
    average = lax.optimization_barrier(jnp.mean(values, axis=-1, keepdims=True))
    centred = values - average
    variance = lax.optimization_barrier(jnp.mean(centred * centred, axis=-1, keepdims=True))
    return centred * lax.rsqrt(variance + NORM_EPS) * norm_gain

def windows_attend(block, heads_count, norm_gain, inward, outward, row_start, total_rows):
    rows_here, cols_here, width = block.shape
    head_dim = width // heads_count
    normed = layer_norm(block.astype(jnp.float32), norm_gain).astype(jnp.bfloat16)
    projected = jnp.dot(normed.reshape(-1, width), inward, preferred_element_type=jnp.float32).astype(jnp.bfloat16)
    tiles = projected.reshape(rows_here // WIN_R, WIN_R, cols_here // WIN_C, WIN_C, 3 * width)
    tiles = tiles.transpose(0, 2, 1, 3, 4).reshape(-1, WIN_R * WIN_C, 3, heads_count, head_dim)
    queries = tiles[:, :, 0].astype(jnp.float32)
    keys = tiles[:, :, 1].astype(jnp.float32)
    values = tiles[:, :, 2].astype(jnp.float32)
    scores = jnp.einsum('nqhd,nkhd->nhqk', queries, keys) * head_dim ** (-0.5)
    row_index = row_start + jnp.arange(rows_here, dtype=jnp.int32)
    region = (row_index >= total_rows - SHIFT_R).astype(jnp.int32)
    labels = jnp.broadcast_to(region[:, None], (rows_here, cols_here))
    labels = labels.reshape(rows_here // WIN_R, WIN_R, cols_here // WIN_C, WIN_C).transpose(0, 2, 1, 3).reshape(-1, WIN_R * WIN_C)
    same_region = labels[:, None, :, None] == labels[:, None, None, :]
    scores = jnp.where(same_region, scores, jnp.float32(-1e+30))
    weights = jax.nn.softmax(scores, axis=-1).astype(jnp.bfloat16)
    context = jnp.einsum('nhqk,nkhd->nqhd', weights.astype(jnp.float32), values).astype(jnp.bfloat16)
    mixed = jnp.dot(context.reshape(-1, width), outward, preferred_element_type=jnp.float32)
    mixed = mixed.reshape(rows_here // WIN_R, cols_here // WIN_C, WIN_R, WIN_C, width).transpose(0, 2, 1, 3, 4)
    return mixed.reshape(rows_here, cols_here, width)

def attend_grid(grid, heads_count, norm_gain, inward, outward):
    total_rows, cols_all, width = grid.shape

    def one_band(band):
        block = lax.dynamic_slice_in_dim(grid, band * WIN_R, WIN_R, 0)
        return windows_attend(block, heads_count, norm_gain, inward, outward, band * WIN_R, total_rows)
    bands = lax.map(one_band, jnp.arange(total_rows // WIN_R, dtype=jnp.int32))
    return bands.reshape(total_rows, cols_all, width)

def feed_grid(grid, norm_gain, expand_weight, reduce_weight):
    total_rows, cols_all, width = grid.shape

    def one_band(band):
        block = lax.dynamic_slice_in_dim(grid, band * WIN_R, WIN_R, 0).reshape(-1, width)
        normed = layer_norm(block.astype(jnp.float32), norm_gain).astype(jnp.bfloat16)
        hidden = jnp.dot(normed, expand_weight, preferred_element_type=jnp.float32)
        hidden = jax.nn.gelu(hidden, approximate=False).astype(jnp.bfloat16)
        result = block.astype(jnp.float32) + jnp.dot(hidden, reduce_weight, preferred_element_type=jnp.float32)
        return result.astype(jnp.bfloat16).reshape(WIN_R, cols_all, width)
    bands = lax.map(one_band, jnp.arange(total_rows // WIN_R, dtype=jnp.int32))
    return bands.reshape(total_rows, cols_all, width)

def merge_pairs(grid, norm_gain, weight):
    joined = jnp.concatenate([grid[0::2, 0::2], grid[1::2, 0::2], grid[0::2, 1::2], grid[1::2, 1::2]], axis=-1)
    rows_half, cols_half, width = joined.shape
    normed = layer_norm(joined.astype(jnp.float32), norm_gain).astype(jnp.bfloat16)
    merged = jnp.dot(normed.reshape(-1, width), weight, preferred_element_type=jnp.float32).astype(jnp.bfloat16)
    return merged.reshape(rows_half, cols_half, weight.shape[1])

def reference(tokens, attend_gain, attend_inward, attend_outward, expand_gain, expand_weight, reduce_weight, merge_gain, merge_weight, coarse_gain, coarse_inward, coarse_outward):
    rolled = jnp.roll(tokens, (-SHIFT_R, -SHIFT_C), (0, 1))
    first = (rolled.astype(jnp.float32) + attend_grid(rolled, HEADS1, attend_gain, attend_inward, attend_outward)).astype(jnp.bfloat16)
    first = jnp.roll(first, (SHIFT_R, SHIFT_C), (0, 1))
    fine = feed_grid(first, expand_gain, expand_weight, reduce_weight)
    merged = merge_pairs(fine, merge_gain, merge_weight)
    rolled_coarse = jnp.roll(merged, (-SHIFT_R, -SHIFT_C), (0, 1))
    coarse = (rolled_coarse.astype(jnp.float32) + attend_grid(rolled_coarse, HEADS2, coarse_gain, coarse_inward, coarse_outward)).astype(jnp.bfloat16)
    return jnp.roll(coarse, (SHIFT_R, SHIFT_C), (0, 1))
```

```python
import functools

import jax
import jax.numpy as jnp
import numpy as np
from jax import lax
from jax.experimental import pallas as pl
from jax.experimental.pallas import tpu as pltpu
from jax.sharding import PartitionSpec as P

EPS = 1e-05
F32, BF16 = jnp.float32, jnp.bfloat16
MESH = pl.DeviceIdType.MESH
PAD = 80
SCALE = 0.125 * 1.4426950408889634
TAIL = (
    -0.9999952912330627,
    -1.1512510776519775,
    -0.4584643542766571,
    -0.053960103541612625,
    0.008507910184562206,
    -0.0009305300191044807,
    6.159897748148069e-05,
    -1.8348464436712675e-06,
)


ARGS = ("tokens", "g1", "wi", "wo", "g2", "we", "wr", "gm", "wm", "gc", "ci", "co")
TABLES = ("own1", "halo1", "east1", "east2", "join", "leave", "stay", "enter")
BUFFERS = (
    "x", "xe", "c", "fine", "fe", "fc", "s", "z", "w", "qkv", "ctx", "hid", "xw", "qkv1", "ctx1",
    "xn2", "acc",
)
HELD = ("wi", "wo", "we", "wr", "wm", *TABLES)
SEMAPHORES = ("lsem", "hsend", "hrecv", "gsend", "grecv")
NAMES = (*ARGS, *TABLES, "out", *BUFFERS, *("v" + n for n in HELD), *SEMAPHORES)
ORDER = (
    "east1", "own1", "wi", "halo1", "wo", "we", "wr", "east2", "join", "wm",
    "leave", "stay", "enter",
)


def one_hot(rows, cols, pairs):
    table = np.zeros((rows, cols), np.float32)
    for r, c in pairs:
        table[r, c] = 1.0
    return table.astype(jnp.bfloat16)


def window_slot(row, col, across):
    return ((row // 6) * across + col // 12) * PAD + (row % 6) * 12 + col % 12


def tables():
    band = [(r, c) for r in range(6) for c in range(48)]
    own1 = one_hot(
        320, 288, [(window_slot(r, c, 4), r * 48 + c + 6) for r, c in band if c < 42]
    )
    halo1 = np.stack(
        [
            one_hot(
                320,
                64,
                [
                    (window_slot(r, c, 4), (6 * b + 3 + r) * 6 + c - 42 - (32 * b + 16))
                    for r, c in band
                    if c >= 42
                ],
            )
            for b in range(4)
        ]
    )
    east1 = one_hot(48, 384, [(r * 6 + c, r * 48 + c) for r in range(8) for c in range(6)])
    east2 = one_hot(144, 320, [((6 * b + r) * 6 + c, b * PAD + r * 12 + c) for b in range(4) for r in range(6) for c in range(6)])
    grid = [(r, c) for r in range(12) for c in range(24)]
    joins = []
    for a in range(2):
        pairs = []
        for r in range(6):
            for c in range(24):
                for part in range(4):
                    row = 2 * (6 * a + r + 1) + 1 + part % 2
                    col = 2 * (c + 3) + part // 2
                    if col < 48:
                        src = window_slot(row - 12 * a, col, 4)
                    else:
                        src = 960 + row * 6 + col - 48 - (16, 80)[a]
                    pairs.append((part * 160 + window_slot(r, c, 2), src))
        joins.append(one_hot(640, 1056, pairs))
    join = np.stack(joins)
    leave = one_hot(
        160,
        320,
        [((r - 9) * 18 + c, window_slot(r, c, 2)) for r in range(9, 12) for c in range(18)]
        + [(64 + r * 6 + c - 18, window_slot(r, c, 2)) for r in range(9) for c in range(18, 24)]
        + [
            (128 + (r - 9) * 6 + c - 18, window_slot(r, c, 2))
            for r in range(9, 12)
            for c in range(18, 24)
        ],
    )
    stay = one_hot(
        288,
        320,
        [(r * 24 + c, window_slot(r - 3, c - 6, 2)) for r, c in grid if r >= 3 and c >= 6],
    )
    enter = one_hot(
        288,
        160,
        [(r * 24 + c, r * 18 + c - 6) for r, c in grid if r < 3 and c >= 6]
        + [(r * 24 + c, 64 + (r - 3) * 6 + c) for r, c in grid if r >= 3 and c < 6]
        + [(r * 24 + c, 128 + r * 6 + c) for r, c in grid if r < 3 and c < 6],
    )
    return own1, halo1, east1, east2, join, leave, stay, enter


def mm(a, b):
    return jnp.dot(a, b, preferred_element_type=F32)


def norm(v, gain):
    centred = v - jnp.mean(v, axis=-1, keepdims=True)
    variance = jnp.mean(centred * centred, axis=-1, keepdims=True)
    return (centred * lax.rsqrt(variance + EPS) * gain).astype(BF16)


def gelu(x):
    a = jnp.abs(x)
    e = jnp.full_like(x, TAIL[-1])
    for c in TAIL[-2::-1]:
        e = e * a + c
    return jnp.maximum(x, 0.0) - a * jnp.exp2(e)


def key_bias(cut):
    q = lax.broadcasted_iota(jnp.int32, (PAD, PAD), 0)
    k = lax.broadcasted_iota(jnp.int32, (PAD, PAD), 1)
    hidden = k >= 72
    if cut is not None:
        hidden = hidden | (cut & ((q >= 36) != (k >= 36)))
    one = jnp.where(hidden, jnp.float32(-1e30), jnp.float32(0.0))
    return jnp.concatenate([one] * 4, axis=0)


def attend_window(qkv, ctx, row, bias, width):
    lane = lax.broadcasted_iota(jnp.int32, (PAD, 256), 1) // 64
    low = lax.broadcasted_iota(jnp.int32, (PAD, 128), 1) < 64
    rows = pl.ds(row, PAD)
    for quad in range(width // 256):
        at = quad * 256
        q = qkv[rows, at : at + 256]
        k = qkv[rows, width + at : width + at + 256]
        v = qkv[rows, 2 * width + at : 2 * width + at + 256]
        q4 = jnp.concatenate([q * (lane == h).astype(BF16) for h in range(4)], axis=0)
        s = lax.dot_general(q4, k, (((1,), (1,)), ((), ())), preferred_element_type=F32) + bias
        p = jnp.exp2((s - jnp.max(s, axis=-1, keepdims=True)) * SCALE)
        total = jnp.sum(p, axis=-1, keepdims=True)
        o = mm(p.astype(BF16), v) * (1.0 / total)
        left = jnp.where(low, o[0:PAD, 0:128], o[PAD : 2 * PAD, 0:128])
        right = jnp.where(low, o[2 * PAD : 3 * PAD, 128:256], o[3 * PAD :, 128:256])
        ctx[rows, at : at + 128] = left.astype(BF16)
        ctx[rows, at + 128 : at + 256] = right.astype(BF16)


def kernel(remote, *refs):
    r = dict(zip(NAMES, refs, strict=True))
    x, xe, c, fine, fe, fc, s, z, w, qkv, ctx, hid, xw, qkv1, ctx1, xn2, acc = (
        r[n] for n in BUFFERS
    )

    lat, lon = lax.axis_index("lat"), lax.axis_index("lon")
    lats, lons = lax.axis_size("lat"), lax.axis_size("lon")
    zs = max(lons // 4, 1)
    y_lo, core = lat % 2, lon % 2
    zi, y_hi = (lon // 2) % zs, lon // (2 * zs)
    north, south = (lat + lats - 1) % lats, (lat + 1) % lats
    west, east = (lon + lons - 1) % lons, (lon + 1) % lons

    def at_z(k):
        return y_hi * (2 * zs) + ((zi + k + zs) % zs) * 2 + core

    other = (lat - y_lo + (1 - y_lo), (1 - y_hi) * (2 * zs) + zi * 2 + core)
    next_x, last_x = ((lat + 2) % lats, lon), ((lat + lats - 2) % lats, lon)
    twin = (lat, lon - core + (1 - core))
    up_z, down_z = (lat, at_z(1)), (lat, at_z(-1))

    def load(i, src, dst):
        copy = pltpu.make_async_copy(src, dst, r["lsem"].at[i])
        copy.start()
        return copy

    shard = pl.ds(pl.multiple_of(lon * 32, 32), 32)
    load_x = load(0, r["tokens"], x.at[pl.ds(0, 1152)])
    load_ci = load(1, r["ci"], w.at[shard, pl.ds(0, 3072)])
    load_co = load(2, r["co"], w.at[shard, pl.ds(3072, 1024)])
    loads = {}

    def fetch(*which):
        for n in which:
            loads[n] = load(3 + ORDER.index(n), r[n], r["v" + n])

    fetch("east1", "own1", "wi")

    def need(*which):
        for n in which:
            loads.pop(n).wait()

    if remote:
        barrier = pltpu.get_barrier_semaphore()
        partners = [
            (north, lon), (south, lon), (lat, west), (lat, east), (north, west), (south, east),
            up_z, down_z, other, next_x, last_x, twin,
        ]
        for partner in partners:
            pl.semaphore_signal(barrier, inc=1, device_id=partner, device_id_type=MESH)

    def send(pair, i, src, dst, device):
        copy = pltpu.make_async_remote_copy(
            src_ref=src, dst_ref=dst, send_sem=r[pair + "send"].at[i],
            recv_sem=r[pair + "recv"].at[i], device_id=device, device_id_type=MESH,
        )
        if remote:
            copy.start()
        return copy

    sent = []

    def halo(i, src, dst, device):
        copy = send("h", i, src, dst, device)
        sent.append(copy)
        return copy

    def arrive(*copies):
        if remote:
            for copy in copies:
                copy.wait_recv()

    seq = [0, -1, 1, -2, 2, -3, 3, 4]
    pick = (lat // 2) % 2

    def rows_of(half, k, start=0, count=32):
        first = (half * (2 * zs) + ((zi + k + zs) % zs) * 2 + core) * 32 + start
        return w.at[pl.ds(pl.multiple_of(first, 16), count)]

    got = {}

    def push(key, i, ref, device):
        got[key] = send("g", i, ref, ref, device)
        sent.append(got[key])

    def half(k, part):
        return rows_of(y_hi, k, 16 * ((pick + part) % 2), 16)

    def push_up(step, part):
        push(("up", step, part), 2 * step + part, half(-step, part), up_z)

    def push_down(step, part):
        i = 7 + (6 if step == 3 else 2 * step + part)
        push(("down", step, part), i, half(step, part), down_z)

    def push_other(n):
        push(("other", n), 14 + n, half(seq[n], 0), other)

    def push_x(n):
        arrive(got["other", n])
        mine = rows_of(1 - y_hi, seq[n], 16 * pick, 16)
        push(("left", n), 22 + 2 * n, mine.at[:, pl.ds(0, 2048)], last_x)
        push(("right", n), 23 + 2 * n, mine.at[:, pl.ds(2048, 2048)], next_x)

    def push_near(n):
        push(("near", n), 38 + n, rows_of(y_hi, seq[n]), twin)

    def push_far(n):
        arrive(got["left", n], got["right", n])
        push(("far", n), 46 + n, rows_of(1 - y_hi, seq[n]), twin)

    def gather_round(j):
        if j == 0:
            load_ci.wait()
            load_co.wait()
            for part in range(2):
                push_up(0, part)
                push_down(0, part)
            push_other(0)
            push_near(0)
        elif j <= 6:
            step, part = (j - 1) // 2, (j - 1) % 2
            arrive(got["up", step, part])
            if step < 2 or part == 0:
                push_up(step + 1, part)
            arrive(got["down", step, part])
            if step < 2 or part == 1:
                push_down(step + 1, part)
            for n in (2 * step + 1, 2 * step + 2):
                push_near(n) if part else push_other(n)
        elif j == 7:
            arrive(got["up", 3, 0])
            push_other(7)
            arrive(got["down", 3, 1])
            push_near(7)
        if 1 <= j <= 8:
            push_x(j - 1)
        if 2 <= j <= 9:
            push_far(j - 2)
        if j == 10:
            arrive(*(got["near", n] for n in range(8)))
        if j == 11:
            arrive(*(got["far", n] for n in range(8)))

    ticks = []

    def tick():
        for j in PLAN.get(len(ticks), ()):
            gather_round(j)
        ticks.append(0)

    plain = key_bias(None)
    seam = key_bias(lat == lats - 1)
    load_x.wait()
    need("east1")
    for g in range(3):
        c[48 * g : 48 * g + 48] = mm(
            r["veast1"][...], x[384 * g : 384 * g + 384]
        ).astype(BF16)
    if remote:
        pl.semaphore_wait(barrier, len(partners))
    row_in = halo(0, x.at[pl.ds(0, 144)], x.at[pl.ds(1152, 144)], (north, lon))
    col_in = halo(1, c, xe.at[pl.ds(0, 144)], (lat, west))
    end_in = halo(2, c.at[pl.ds(0, 32)], xe.at[pl.ds(144, 32)], (north, west))
    gather_round(0)
    fetch("halo1", "wo", "we", "wr")

    fine[16:20, 48:80] = jnp.zeros((4, 32, 512), BF16)

    need("own1", "wi")
    for b in range(3):
        at = slice(320 * b, 320 * b + 240)
        wx = mm(r["vown1"][0:240], x[(6 * b + 3) * 48 : (6 * b + 9) * 48])
        xw[at] = wx.astype(BF16)
        qkv1[at] = mm(norm(wx, r["g1"][...]), r["vwi"][...]).astype(BF16)
        for k in range(3):
            attend_window(qkv1, ctx1, 320 * b + k * PAD, plain, 512)
        tick()

    fetch("east2", "join", "wm", "leave", "stay", "enter")
    arrive(row_in, col_in, end_in)
    need("halo1")
    edges = []
    for b in range(4):
        part = slice(240, 320) if b < 3 else slice(0, 320)
        wx = mm(r["vown1"][part], x[(6 * b + 3) * 48 : (6 * b + 9) * 48])
        wx = wx + mm(r["vhalo1"][b, part], xe[32 * b + 16 : 32 * b + 80])
        xw[320 * b + part.start : 320 * b + 320] = wx.astype(BF16)
        edges.append(norm(wx, r["g1"][...]))
    edges = jnp.concatenate(edges, axis=0)
    for j in range(3):
        some = slice(512 * j, 512 * j + 512)
        made = mm(edges, r["vwi"][:, some]).astype(BF16)
        for b in range(3):
            qkv1[320 * b + 240 : 320 * b + 320, some] = made[80 * b : 80 * b + 80]
        qkv1[960:1280, some] = made[240:560]
    tick()
    for b in range(3):
        attend_window(qkv1, ctx1, 320 * b + 240, plain, 512)
    tick()
    for k in range(4):
        attend_window(qkv1, ctx1, 960 + k * PAD, seam, 512)
    tick()
    need("wo", "we", "wr")

    def feed(slots):
        parts = []
        for start, count in slots:
            at = slice(PAD * start, PAD * (start + count))
            first = xw[at].astype(F32) + mm(ctx1[at], r["vwo"][...])
            parts += [first[PAD * k : PAD * k + 72] for k in range(count)]
        f = jnp.concatenate(parts, axis=0).astype(BF16).astype(F32)
        fn = norm(f, r["g2"][...])
        size = f.shape[0]
        for j in range(4):
            some = slice(512 * j, 512 * j + 512)
            hid[0:size, some] = gelu(mm(fn, r["vwe"][:, some])).astype(BF16)
            tick()
        total = f + mm(hid[0:size], r["vwr"][...])
        blank = jnp.zeros((PAD - 72, 512), F32)
        at = 0
        for start, count in slots:
            for k in range(count):
                whole = jnp.concatenate([total[at : at + 72], blank], axis=0)
                fine[start + k] = whole.astype(BF16)
                at += 72
        tick()

    feed([(0, 4), (4, 1), (8, 1), (12, 1)])
    need("east2")
    west_edge = jnp.concatenate([fine[4 * b] for b in range(4)], axis=0)
    fc[...] = mm(r["veast2"][...], west_edge).astype(BF16)
    row_in = halo(
        3, fine.at[pl.ds(0, 4), pl.ds(0, 48)], fine.at[pl.ds(16, 4), pl.ds(0, 48)], (north, lon)
    )
    col_in = halo(4, fc, fe.at[pl.ds(0, 144)], (lat, west))
    end_in = halo(5, fc.at[pl.ds(0, 32)], fe.at[pl.ds(144, 32)], (north, west))
    feed([(5, 3), (9, 3), (13, 3)])

    need("join", "wm")
    arrive(row_in, col_in, end_in)
    blocks = []
    for a in range(2):
        bands = fine[8 * a : 8 * a + 12].reshape(960, 512)
        start = (16, 80)[a]
        blocks.append(
            mm(r["vjoin"][a, :, 0:960], bands)
            + mm(r["vjoin"][a, :, 960:1056], fe[start : start + 96])
        )
    members = [
        jnp.concatenate([blocks[a][160 * k : 160 * k + 160] for a in range(2)], axis=0)
        for k in range(4)
    ]
    tick()
    mean = sum(jnp.sum(v, -1, keepdims=True) for v in members) * (1 / 2048)
    members = [v - mean for v in members]
    factor = lax.rsqrt(
        sum(jnp.sum(v * v, -1, keepdims=True) for v in members) * (1 / 2048) + EPS
    )
    joined = jnp.concatenate(
        [
            (v * factor * r["gm"][:, 512 * k : 512 * k + 512]).astype(BF16)
            for k, v in enumerate(members)
        ],
        axis=1,
    )
    wx = mm(joined, r["vwm"][...]).astype(BF16).astype(F32)
    tick()

    need("leave", "stay", "enter")
    xn = norm(wx, r["gc"][...])
    xn2[0] = xn[:, 0:512]
    xn2[1] = xn[:, 512:1024]
    depth = w.shape[0] // 2
    near = pl.ds(pl.multiple_of(y_hi * depth, depth), depth)
    far = pl.ds(pl.multiple_of((1 - y_hi) * depth, depth), depth)
    for j in range(6):
        some = slice(512 * j, 512 * j + 512)
        acc[:, some] = mm(xn2[y_hi], w[near, some])
        tick()
    for j in range(6):
        some = slice(512 * j, 512 * j + 512)
        qkv[:, some] = (acc[:, some] + mm(xn2[1 - y_hi], w[far, some])).astype(BF16)
    for k in (1, 2, 3, 0):
        attend_window(qkv, ctx, k * PAD, seam if k >= 2 else plain, 1024)
    y = (wx + mm(ctx[...], w[:, 3072:4096])).astype(BF16)
    s[...] = mm(r["vleave"][...], y).astype(BF16)
    row_back = halo(6, s.at[pl.ds(0, 64)], z.at[pl.ds(0, 64)], (south, lon))
    col_back = halo(7, s.at[pl.ds(64, 64)], z.at[pl.ds(64, 64)], (lat, east))
    end_back = halo(8, s.at[pl.ds(128, 32)], z.at[pl.ds(128, 32)], (south, east))
    kept = mm(r["vstay"][...], y)
    arrive(row_back, col_back, end_back)
    r["out"][...] = (kept + mm(r["venter"][...], z[...])).astype(BF16)
    if remote:
        for copy in sent:
            copy.wait_send()


PLAN = {
    2: (1,), 4: (2,), 6: (3,), 9: (4,), 11: (5,), 14: (6,), 15: (7,), 16: (8,), 17: (10, 9),
    23: (11,),
}


def per_device(remote, *args):
    tokens, g1, wi, wo, g2, we, wr, gm, wm, gc, ci, co = args
    consts = [jnp.asarray(t) for t in tables()]
    operands = [
        tokens.reshape(1152, 512), g1.reshape(1, -1), wi, wo, g2.reshape(1, -1), we, wr,
        gm.reshape(1, -1), wm, gc.reshape(1, -1), ci, co, *consts,
    ]
    hbm = pl.BlockSpec(memory_space=pl.ANY)
    vmem = pl.BlockSpec(memory_space=pltpu.VMEM)
    small = (1, 4, 7, 9)
    held = [wi, wo, we, wr, wm, *consts]
    scratch = [
        pltpu.VMEM((1296, 512), BF16),
        pltpu.VMEM((176, 512), BF16),
        pltpu.VMEM((144, 512), BF16),
        pltpu.VMEM((20, PAD, 512), BF16),
        pltpu.VMEM((176, 512), BF16),
        pltpu.VMEM((144, 512), BF16),
        pltpu.VMEM((160, 1024), BF16),
        pltpu.VMEM((160, 1024), BF16),
        pltpu.VMEM((1024, 4096), BF16),
        pltpu.VMEM((320, 3072), BF16),
        pltpu.VMEM((320, 1024), BF16),
        pltpu.VMEM((648, 2048), BF16),
        pltpu.VMEM((1280, 512), BF16),
        pltpu.VMEM((1280, 1536), BF16),
        pltpu.VMEM((1280, 512), BF16),
        pltpu.VMEM((2, 320, 512), BF16),
        pltpu.VMEM((320, 3072), F32),
        *(pltpu.VMEM(a.shape, BF16) for a in held),
        pltpu.SemaphoreType.DMA((3 + len(ORDER),)),
        pltpu.SemaphoreType.DMA((10,)),
        pltpu.SemaphoreType.DMA((10,)),
        pltpu.SemaphoreType.DMA((54,)),
        pltpu.SemaphoreType.DMA((54,)),
    ]
    params = dict(collective_id=0, has_side_effects=True) if remote else {}
    out = pl.pallas_call(
        functools.partial(kernel, remote),
        out_shape=jax.ShapeDtypeStruct((288, 1024), BF16),
        in_specs=[vmem if i in small else hbm for i in range(len(operands))],
        out_specs=vmem,
        scratch_shapes=scratch,
        compiler_params=pltpu.CompilerParams(vmem_limit_bytes=60 * 1024 * 1024, **params),
        name="encoder",
    )(*operands)
    return out.reshape(12, 24, 1024)


def solution(mesh, remote=True):
    return jax.shard_map(
        functools.partial(per_device, remote),
        mesh=mesh,
        in_specs=(P("lat", "lon", None), *[P()] * 9, P("lon", None), P("lon", None)),
        out_specs=P("lat", "lon", None),
        check_vma=False,
    )
```

```python
import functools

import jax
import jax.numpy as jnp
import numpy as np
from jax import lax
from jax.experimental import pallas as pl
from jax.experimental.pallas import tpu as pltpu
from jax.sharding import PartitionSpec as P

EPS = 1e-05
F32, BF16 = jnp.float32, jnp.bfloat16
MESH = pl.DeviceIdType.MESH
PAD = 80
SCALE = 0.125 * 1.4426950408889634
TAIL = (
    -0.9999952912330627,
    -1.1512510776519775,
    -0.4584643542766571,
    -0.053960103541612625,
    0.008507910184562206,
    -0.0009305300191044807,
    6.159897748148069e-05,
    -1.8348464436712675e-06,
)


ARGS = ("tokens", "g1", "wi", "wo", "g2", "we", "wr", "gm", "wm", "gc", "ci", "co")
TABLES = ("own1", "halo1", "east1", "east2", "join", "leave", "stay", "enter")
BUFFERS = (
    "x", "xe", "c", "fine", "fe", "fc", "s", "z", "w", "qkv", "ctx", "hid", "xw", "qkv1", "ctx1",
    "xn2", "acc",
)
HELD = ("wi", "wo", "we", "wr", "wm", *TABLES)
SEMAPHORES = ("lsem", "hsend", "hrecv", "gsend", "grecv")
NAMES = (*ARGS, *TABLES, "out", *BUFFERS, *("v" + n for n in HELD), *SEMAPHORES)
ORDER = (
    "east1", "own1", "wi", "halo1", "wo", "we", "wr", "east2", "join", "wm",
    "leave", "stay", "enter",
)


def one_hot(rows, cols, pairs):
    table = np.zeros((rows, cols), np.float32)
    for r, c in pairs:
        table[r, c] = 1.0
    return table.astype(jnp.bfloat16)


def window_slot(row, col, across):
    return ((row // 6) * across + col // 12) * PAD + (row % 6) * 12 + col % 12


def tables():
    band = [(r, c) for r in range(6) for c in range(48)]
    own1 = one_hot(
        320, 288, [(window_slot(r, c, 4), r * 48 + c + 6) for r, c in band if c < 42]
    )
    halo1 = np.stack(
        [
            one_hot(
                320,
                64,
                [
                    (window_slot(r, c, 4), (6 * b + 3 + r) * 6 + c - 42 - (32 * b + 16))
                    for r, c in band
                    if c >= 42
                ],
            )
            for b in range(4)
        ]
    )
    east1 = one_hot(48, 384, [(r * 6 + c, r * 48 + c) for r in range(8) for c in range(6)])
    east2 = one_hot(144, 320, [((6 * b + r) * 6 + c, b * PAD + r * 12 + c) for b in range(4) for r in range(6) for c in range(6)])
    grid = [(r, c) for r in range(12) for c in range(24)]
    joins = []
    for a in range(2):
        pairs = []
        for r in range(6):
            for c in range(24):
                for part in range(4):
                    row = 2 * (6 * a + r + 1) + 1 + part % 2
                    col = 2 * (c + 3) + part // 2
                    if col < 48:
                        src = window_slot(row - 12 * a, col, 4)
                    else:
                        src = 960 + row * 6 + col - 48 - (16, 80)[a]
                    pairs.append((part * 160 + window_slot(r, c, 2), src))
        joins.append(one_hot(640, 1056, pairs))
    join = np.stack(joins)
    leave = one_hot(
        160,
        240,
        [((r - 9) * 18 + c, window_slot(r, c, 2) - PAD) for r in range(9, 12) for c in range(18)]
        + [(64 + r * 6 + c - 18, window_slot(r, c, 2) - PAD) for r in range(9) for c in range(18, 24)]
        + [
            (128 + (r - 9) * 6 + c - 18, window_slot(r, c, 2) - PAD)
            for r in range(9, 12)
            for c in range(18, 24)
        ],
    )
    stay = one_hot(
        288,
        320,
        [(r * 24 + c, window_slot(r - 3, c - 6, 2)) for r, c in grid if r >= 3 and c >= 6],
    )
    enter = one_hot(
        288,
        160,
        [(r * 24 + c, r * 18 + c - 6) for r, c in grid if r < 3 and c >= 6]
        + [(r * 24 + c, 64 + (r - 3) * 6 + c) for r, c in grid if r >= 3 and c < 6]
        + [(r * 24 + c, 128 + r * 6 + c) for r, c in grid if r < 3 and c < 6],
    )
    return own1, halo1, east1, east2, join, leave, stay, enter


def mm(a, b):
    return jnp.dot(a, b, preferred_element_type=F32)


def norm(v, gain):
    centred = v - jnp.mean(v, axis=-1, keepdims=True)
    variance = jnp.mean(centred * centred, axis=-1, keepdims=True)
    return (centred * lax.rsqrt(variance + EPS) * gain).astype(BF16)


def gelu(x):
    a = jnp.abs(x)
    e = jnp.full_like(x, TAIL[-1])
    for c in TAIL[-2::-1]:
        e = e * a + c
    return jnp.maximum(x, 0.0) - a * jnp.exp2(e)


def key_bias(cut):
    q = lax.broadcasted_iota(jnp.int32, (PAD, PAD), 0)
    k = lax.broadcasted_iota(jnp.int32, (PAD, PAD), 1)
    hidden = k >= 72
    if cut is not None:
        hidden = hidden | (cut & ((q >= 36) != (k >= 36)))
    one = jnp.where(hidden, jnp.float32(-1e30), jnp.float32(0.0))
    return jnp.concatenate([one] * 4, axis=0)


def attend_window(qkv, ctx, row, bias, width):
    lane = lax.broadcasted_iota(jnp.int32, (PAD, 256), 1) // 64
    low = lax.broadcasted_iota(jnp.int32, (PAD, 128), 1) < 64
    rows = pl.ds(row, PAD)
    for quad in range(width // 256):
        at = quad * 256
        q = qkv[rows, at : at + 256]
        k = qkv[rows, width + at : width + at + 256]
        v = qkv[rows, 2 * width + at : 2 * width + at + 256]
        q4 = jnp.concatenate([q * (lane == h).astype(BF16) for h in range(4)], axis=0)
        s = lax.dot_general(q4, k, (((1,), (1,)), ((), ())), preferred_element_type=F32) + bias
        p = jnp.exp2((s - jnp.max(s, axis=-1, keepdims=True)) * SCALE)
        total = jnp.sum(p, axis=-1, keepdims=True)
        o = mm(p.astype(BF16), v) * (1.0 / total)
        left = jnp.where(low, o[0:PAD, 0:128], o[PAD : 2 * PAD, 0:128])
        right = jnp.where(low, o[2 * PAD : 3 * PAD, 128:256], o[3 * PAD :, 128:256])
        ctx[rows, at : at + 128] = left.astype(BF16)
        ctx[rows, at + 128 : at + 256] = right.astype(BF16)


def kernel(remote, *refs):
    r = dict(zip(NAMES, refs, strict=True))
    x, xe, c, fine, fe, fc, s, z, w, qkv, ctx, hid, xw, qkv1, ctx1, xn2, acc = (
        r[n] for n in BUFFERS
    )

    lat, lon = lax.axis_index("lat"), lax.axis_index("lon")
    lats, lons = lax.axis_size("lat"), lax.axis_size("lon")
    zs = max(lons // 4, 1)
    y_lo, core = lat % 2, lon % 2
    zi, y_hi = (lon // 2) % zs, lon // (2 * zs)
    north, south = (lat + lats - 1) % lats, (lat + 1) % lats
    west, east = (lon + lons - 1) % lons, (lon + 1) % lons

    def at_z(k):
        return y_hi * (2 * zs) + ((zi + k + zs) % zs) * 2 + core

    other = (lat - y_lo + (1 - y_lo), (1 - y_hi) * (2 * zs) + zi * 2 + core)
    next_x, last_x = ((lat + 2) % lats, lon), ((lat + lats - 2) % lats, lon)
    twin = (lat, lon - core + (1 - core))
    up_z, down_z = (lat, at_z(1)), (lat, at_z(-1))

    def load(i, src, dst):
        copy = pltpu.make_async_copy(src, dst, r["lsem"].at[i])
        copy.start()
        return copy

    shard = pl.ds(pl.multiple_of(lon * 32, 32), 32)
    load_x = load(0, r["tokens"], x.at[pl.ds(0, 1152)])
    load_ci = load(1, r["ci"], w.at[shard, pl.ds(0, 3072)])
    load_co = load(2, r["co"], w.at[shard, pl.ds(3072, 1024)])
    loads = {}

    def fetch(*which):
        for n in which:
            loads[n] = load(3 + ORDER.index(n), r[n], r["v" + n])

    fetch("east1", "own1", "wi")

    def need(*which):
        for n in which:
            loads.pop(n).wait()

    if remote:
        barrier = pltpu.get_barrier_semaphore()
        partners = [
            (north, lon), (south, lon), (lat, west), (lat, east), (north, west), (south, east),
            up_z, down_z, other, next_x, last_x, twin,
        ]
        for partner in partners:
            pl.semaphore_signal(barrier, inc=1, device_id=partner, device_id_type=MESH)

    def send(pair, i, src, dst, device):
        copy = pltpu.make_async_remote_copy(
            src_ref=src, dst_ref=dst, send_sem=r[pair + "send"].at[i],
            recv_sem=r[pair + "recv"].at[i], device_id=device, device_id_type=MESH,
        )
        if remote:
            copy.start()
        return copy

    sent = []

    def halo(i, src, dst, device):
        copy = send("h", i, src, dst, device)
        sent.append(copy)
        return copy

    def arrive(*copies):
        if remote:
            for copy in copies:
                copy.wait_recv()

    seq = [0, -1, 1, -2, 2, -3, 3, 4]
    pick = (lat // 2) % 2

    def rows_of(half, k, start=0, count=32):
        first = (half * (2 * zs) + ((zi + k + zs) % zs) * 2 + core) * 32 + start
        return w.at[pl.ds(pl.multiple_of(first, 16), count)]

    got = {}

    def push(key, i, ref, device):
        got[key] = send("g", i, ref, ref, device)
        sent.append(got[key])

    def half(k, part):
        return rows_of(y_hi, k, 16 * ((pick + part) % 2), 16)

    def push_up(step, part):
        push(("up", step, part), 2 * step + part, half(-step, part), up_z)

    def push_down(step, part):
        i = 7 + (6 if step == 3 else 2 * step + part)
        push(("down", step, part), i, half(step, part), down_z)

    def push_other(n):
        push(("other", n), 14 + n, half(seq[n], 0), other)

    def push_x(n):
        arrive(got["other", n])
        mine = rows_of(1 - y_hi, seq[n], 16 * pick, 16)
        push(("left", n), 22 + 2 * n, mine.at[:, pl.ds(0, 2048)], last_x)
        push(("right", n), 23 + 2 * n, mine.at[:, pl.ds(2048, 2048)], next_x)

    def push_near(n):
        push(("near", n), 38 + n, rows_of(y_hi, seq[n]), twin)

    def push_far(n):
        arrive(got["left", n], got["right", n])
        push(("far", n), 46 + n, rows_of(1 - y_hi, seq[n]), twin)

    def gather_round(j):
        if j == 0:
            load_ci.wait()
            load_co.wait()
            for part in range(2):
                push_up(0, part)
                push_down(0, part)
            push_other(0)
            push_near(0)
        elif j <= 6:
            step, part = (j - 1) // 2, (j - 1) % 2
            arrive(got["up", step, part])
            if step < 2 or part == 0:
                push_up(step + 1, part)
            arrive(got["down", step, part])
            if step < 2 or part == 1:
                push_down(step + 1, part)
            for n in (2 * step + 1, 2 * step + 2):
                push_near(n) if part else push_other(n)
        elif j == 7:
            arrive(got["up", 3, 0])
            push_other(7)
            arrive(got["down", 3, 1])
            push_near(7)
        if 1 <= j <= 8:
            push_x(j - 1)
        if 2 <= j <= 9:
            push_far(j - 2)
        if j == 10:
            arrive(*(got["near", n] for n in range(8)))
        if j == 11:
            arrive(*(got["far", n] for n in range(8)))

    ticks = []

    def tick():
        for j in PLAN.get(len(ticks), ()):
            gather_round(j)
        ticks.append(0)

    plain = key_bias(None)
    seam = key_bias(lat == lats - 1)
    load_x.wait()
    need("east1")
    for g in range(3):
        c[48 * g : 48 * g + 48] = mm(
            r["veast1"][...], x[384 * g : 384 * g + 384]
        ).astype(BF16)
    if remote:
        pl.semaphore_wait(barrier, len(partners))
    row_in = halo(0, x.at[pl.ds(0, 144)], x.at[pl.ds(1152, 144)], (north, lon))
    col_in = halo(1, c, xe.at[pl.ds(0, 144)], (lat, west))
    end_in = halo(2, c.at[pl.ds(0, 32)], xe.at[pl.ds(144, 32)], (north, west))
    gather_round(0)
    fetch("halo1", "wo", "we", "wr")

    fine[16:20, 48:80] = jnp.zeros((4, 32, 512), BF16)

    need("own1", "wi")
    for b in range(3):
        at = slice(320 * b, 320 * b + 240)
        wx = mm(r["vown1"][0:240], x[(6 * b + 3) * 48 : (6 * b + 9) * 48])
        xw[at] = wx.astype(BF16)
        qkv1[at] = mm(norm(wx, r["g1"][...]), r["vwi"][...]).astype(BF16)
        for k in range(3):
            attend_window(qkv1, ctx1, 320 * b + k * PAD, plain, 512)
        tick()

    fetch("east2", "join", "wm", "leave", "stay", "enter")
    arrive(row_in, col_in, end_in)
    need("halo1")
    edges = []
    for b in range(4):
        part = slice(240, 320) if b < 3 else slice(0, 320)
        wx = mm(r["vown1"][part], x[(6 * b + 3) * 48 : (6 * b + 9) * 48])
        wx = wx + mm(r["vhalo1"][b, part], xe[32 * b + 16 : 32 * b + 80])
        xw[320 * b + part.start : 320 * b + 320] = wx.astype(BF16)
        edges.append(norm(wx, r["g1"][...]))
    edges = jnp.concatenate(edges, axis=0)
    for j in range(3):
        some = slice(512 * j, 512 * j + 512)
        made = mm(edges, r["vwi"][:, some]).astype(BF16)
        for b in range(3):
            qkv1[320 * b + 240 : 320 * b + 320, some] = made[80 * b : 80 * b + 80]
        qkv1[960:1280, some] = made[240:560]
    tick()
    for b in range(3):
        attend_window(qkv1, ctx1, 320 * b + 240, plain, 512)
    tick()
    for k in range(4):
        attend_window(qkv1, ctx1, 960 + k * PAD, seam, 512)
    tick()
    need("wo", "we", "wr")

    def feed(slots):
        parts = []
        for start, count in slots:
            at = slice(PAD * start, PAD * (start + count))
            first = xw[at].astype(F32) + mm(ctx1[at], r["vwo"][...])
            parts += [first[PAD * k : PAD * k + 72] for k in range(count)]
        f = jnp.concatenate(parts, axis=0).astype(BF16).astype(F32)
        fn = norm(f, r["g2"][...])
        size = f.shape[0]
        for j in range(4):
            some = slice(512 * j, 512 * j + 512)
            hid[0:size, some] = gelu(mm(fn, r["vwe"][:, some])).astype(BF16)
            tick()
        total = f + mm(hid[0:size], r["vwr"][...])
        blank = jnp.zeros((PAD - 72, 512), F32)
        at = 0
        for start, count in slots:
            for k in range(count):
                whole = jnp.concatenate([total[at : at + 72], blank], axis=0)
                fine[start + k] = whole.astype(BF16)
                at += 72
        tick()

    feed([(0, 4), (4, 1), (8, 1), (12, 1)])
    need("east2")
    west_edge = jnp.concatenate([fine[4 * b] for b in range(4)], axis=0)
    fc[...] = mm(r["veast2"][...], west_edge).astype(BF16)
    row_in = halo(
        3, fine.at[pl.ds(0, 4), pl.ds(0, 48)], fine.at[pl.ds(16, 4), pl.ds(0, 48)], (north, lon)
    )
    col_in = halo(4, fc, fe.at[pl.ds(0, 144)], (lat, west))
    end_in = halo(5, fc.at[pl.ds(0, 32)], fe.at[pl.ds(144, 32)], (north, west))
    feed([(5, 3), (9, 3), (13, 3)])

    need("join", "wm")
    arrive(row_in, col_in, end_in)
    blocks = []
    for a in range(2):
        bands = fine[8 * a : 8 * a + 12].reshape(960, 512)
        start = (16, 80)[a]
        blocks.append(
            mm(r["vjoin"][a, :, 0:960], bands)
            + mm(r["vjoin"][a, :, 960:1056], fe[start : start + 96])
        )
    members = [
        jnp.concatenate([blocks[a][160 * k : 160 * k + 160] for a in range(2)], axis=0)
        for k in range(4)
    ]
    tick()
    mean = sum(jnp.sum(v, -1, keepdims=True) for v in members) * (1 / 2048)
    members = [v - mean for v in members]
    factor = lax.rsqrt(
        sum(jnp.sum(v * v, -1, keepdims=True) for v in members) * (1 / 2048) + EPS
    )
    joined = jnp.concatenate(
        [
            (v * factor * r["gm"][:, 512 * k : 512 * k + 512]).astype(BF16)
            for k, v in enumerate(members)
        ],
        axis=1,
    )
    wx = mm(joined, r["vwm"][...]).astype(BF16).astype(F32)
    tick()

    need("leave", "stay", "enter")
    xn = norm(wx, r["gc"][...])
    xn2[0] = xn[:, 0:512]
    xn2[1] = xn[:, 512:1024]
    depth = w.shape[0] // 2
    near = pl.ds(pl.multiple_of(y_hi * depth, depth), depth)
    far = pl.ds(pl.multiple_of((1 - y_hi) * depth, depth), depth)
    for j in range(6):
        some = slice(512 * j, 512 * j + 512)
        acc[:, some] = mm(xn2[y_hi], w[near, some])
        tick()
    for j in range(6):
        some = slice(512 * j, 512 * j + 512)
        qkv[:, some] = (acc[:, some] + mm(xn2[1 - y_hi], w[far, some])).astype(BF16)
    for k in (3, 2, 1):
        attend_window(qkv, ctx, k * PAD, seam if k >= 2 else plain, 1024)
    y_edge = (wx[PAD:] + mm(ctx[PAD:320], w[:, 3072:4096])).astype(BF16)
    s[...] = mm(r["vleave"][...], y_edge).astype(BF16)
    row_back = halo(6, s.at[pl.ds(0, 64)], z.at[pl.ds(0, 64)], (south, lon))
    col_back = halo(7, s.at[pl.ds(64, 64)], z.at[pl.ds(64, 64)], (lat, east))
    end_back = halo(8, s.at[pl.ds(128, 32)], z.at[pl.ds(128, 32)], (south, east))
    attend_window(qkv, ctx, 0, plain, 1024)
    y_rest = (wx[0:PAD] + mm(ctx[0:PAD], w[:, 3072:4096])).astype(BF16)
    kept = mm(r["vstay"][...], jnp.concatenate([y_rest, y_edge], axis=0))
    arrive(row_back, col_back, end_back)
    r["out"][...] = (kept + mm(r["venter"][...], z[...])).astype(BF16)
    if remote:
        for copy in sent:
            copy.wait_send()


PLAN = {
    2: (1,), 4: (2,), 6: (3,), 9: (4,), 11: (5,), 14: (6,), 15: (7,), 16: (8,), 17: (10, 9),
    23: (11,),
}


def per_device(remote, *args):
    tokens, g1, wi, wo, g2, we, wr, gm, wm, gc, ci, co = args
    consts = [jnp.asarray(t) for t in tables()]
    operands = [
        tokens.reshape(1152, 512), g1.reshape(1, -1), wi, wo, g2.reshape(1, -1), we, wr,
        gm.reshape(1, -1), wm, gc.reshape(1, -1), ci, co, *consts,
    ]
    hbm = pl.BlockSpec(memory_space=pl.ANY)
    vmem = pl.BlockSpec(memory_space=pltpu.VMEM)
    small = (1, 4, 7, 9)
    held = [wi, wo, we, wr, wm, *consts]
    scratch = [
        pltpu.VMEM((1296, 512), BF16),
        pltpu.VMEM((176, 512), BF16),
        pltpu.VMEM((144, 512), BF16),
        pltpu.VMEM((20, PAD, 512), BF16),
        pltpu.VMEM((176, 512), BF16),
        pltpu.VMEM((144, 512), BF16),
        pltpu.VMEM((160, 1024), BF16),
        pltpu.VMEM((160, 1024), BF16),
        pltpu.VMEM((1024, 4096), BF16),
        pltpu.VMEM((320, 3072), BF16),
        pltpu.VMEM((320, 1024), BF16),
        pltpu.VMEM((648, 2048), BF16),
        pltpu.VMEM((1280, 512), BF16),
        pltpu.VMEM((1280, 1536), BF16),
        pltpu.VMEM((1280, 512), BF16),
        pltpu.VMEM((2, 320, 512), BF16),
        pltpu.VMEM((320, 3072), F32),
        *(pltpu.VMEM(a.shape, BF16) for a in held),
        pltpu.SemaphoreType.DMA((3 + len(ORDER),)),
        pltpu.SemaphoreType.DMA((10,)),
        pltpu.SemaphoreType.DMA((10,)),
        pltpu.SemaphoreType.DMA((54,)),
        pltpu.SemaphoreType.DMA((54,)),
    ]
    params = dict(collective_id=0, has_side_effects=True) if remote else {}
    out = pl.pallas_call(
        functools.partial(kernel, remote),
        out_shape=jax.ShapeDtypeStruct((288, 1024), BF16),
        in_specs=[vmem if i in small else hbm for i in range(len(operands))],
        out_specs=vmem,
        scratch_shapes=scratch,
        compiler_params=pltpu.CompilerParams(vmem_limit_bytes=60 * 1024 * 1024, **params),
        name="encoder",
    )(*operands)
    return out.reshape(12, 24, 1024)


def solution(mesh, remote=True):
    return jax.shard_map(
        functools.partial(per_device, remote),
        mesh=mesh,
        in_specs=(P("lat", "lon", None), *[P()] * 9, P("lon", None), P("lon", None)),
        out_specs=P("lat", "lon", None),
        check_vma=False,
    )
```

```python
import functools

import jax
import jax.numpy as jnp
import numpy as np
from jax import lax
from jax.experimental import pallas as pl
from jax.experimental.pallas import tpu as pltpu
from jax.sharding import PartitionSpec as P

EPS = 1e-05
F32, BF16 = jnp.float32, jnp.bfloat16
MESH = pl.DeviceIdType.MESH
PAD = 80
SCALE = 0.125 * 1.4426950408889634
TAIL = (
    -0.9999952912330627,
    -1.1512510776519775,
    -0.4584643542766571,
    -0.053960103541612625,
    0.008507910184562206,
    -0.0009305300191044807,
    6.159897748148069e-05,
    -1.8348464436712675e-06,
)


ARGS = ("tokens", "g1", "wi", "wo", "g2", "we", "wr", "gm", "wm", "gc", "ci", "co")
TABLES = ("own1", "halo1", "east1", "east2", "join", "leave", "stay", "enter")
BUFFERS = (
    "x", "xe", "c", "fine", "fe", "fc", "s", "z", "w", "qkv", "ctx", "hid", "xw", "qkv1", "ctx1",
    "xn2", "acc",
)
HELD = ("wi", "wo", "we", "wr", "wm", *TABLES)
SEMAPHORES = ("lsem", "hsend", "hrecv", "gsend", "grecv")
NAMES = (*ARGS, *TABLES, "out", *BUFFERS, *("v" + n for n in HELD), *SEMAPHORES)
ORDER = (
    "east1", "own1", "wi", "halo1", "wo", "we", "wr", "east2", "join", "wm",
    "leave", "stay", "enter",
)


def one_hot(rows, cols, pairs):
    table = np.zeros((rows, cols), np.float32)
    for r, c in pairs:
        table[r, c] = 1.0
    return table.astype(jnp.bfloat16)


def window_slot(row, col, across):
    return ((row // 6) * across + col // 12) * PAD + (row % 6) * 12 + col % 12


def tables():
    band = [(r, c) for r in range(6) for c in range(48)]
    own1 = one_hot(
        320, 288, [(window_slot(r, c, 4), r * 48 + c + 6) for r, c in band if c < 42]
    )
    halo1 = np.stack(
        [
            one_hot(
                320,
                64,
                [
                    (window_slot(r, c, 4), (6 * b + 3 + r) * 6 + c - 42 - (32 * b + 16))
                    for r, c in band
                    if c >= 42
                ],
            )
            for b in range(4)
        ]
    )
    east1 = one_hot(48, 384, [(r * 6 + c, r * 48 + c) for r in range(8) for c in range(6)])
    east2 = one_hot(144, 320, [((6 * b + r) * 6 + c, b * PAD + r * 12 + c) for b in range(4) for r in range(6) for c in range(6)])
    grid = [(r, c) for r in range(12) for c in range(24)]
    joins = []
    for a in range(2):
        pairs = []
        for r in range(6):
            for c in range(24):
                for part in range(4):
                    row = 2 * (6 * a + r + 1) + 1 + part % 2
                    col = 2 * (c + 3) + part // 2
                    if col < 48:
                        src = window_slot(row - 12 * a, col, 4)
                    else:
                        src = 960 + row * 6 + col - 48 - (16, 80)[a]
                    pairs.append((part * 160 + window_slot(r, c, 2), src))
        joins.append(one_hot(640, 1056, pairs))
    join = np.stack(joins)
    leave = one_hot(
        160,
        240,
        [((r - 9) * 18 + c, window_slot(r, c, 2) - PAD) for r in range(9, 12) for c in range(18)]
        + [(64 + r * 6 + c - 18, window_slot(r, c, 2) - PAD) for r in range(9) for c in range(18, 24)]
        + [
            (128 + (r - 9) * 6 + c - 18, window_slot(r, c, 2) - PAD)
            for r in range(9, 12)
            for c in range(18, 24)
        ],
    )
    stay = one_hot(
        288,
        320,
        [(r * 24 + c, window_slot(r - 3, c - 6, 2)) for r, c in grid if r >= 3 and c >= 6],
    )
    enter = one_hot(
        288,
        160,
        [(r * 24 + c, r * 18 + c - 6) for r, c in grid if r < 3 and c >= 6]
        + [(r * 24 + c, 64 + (r - 3) * 6 + c) for r, c in grid if r >= 3 and c < 6]
        + [(r * 24 + c, 128 + r * 6 + c) for r, c in grid if r < 3 and c < 6],
    )
    return own1, halo1, east1, east2, join, leave, stay, enter


def mm(a, b):
    return jnp.dot(a, b, preferred_element_type=F32)


def norm(v, gain):
    centred = v - jnp.mean(v, axis=-1, keepdims=True)
    variance = jnp.mean(centred * centred, axis=-1, keepdims=True)
    return (centred * lax.rsqrt(variance + EPS) * gain).astype(BF16)


def gelu(x):
    a = jnp.abs(x)
    e = jnp.full_like(x, TAIL[-1])
    for c in TAIL[-2::-1]:
        e = e * a + c
    return jnp.maximum(x, 0.0) - a * jnp.exp2(e)


def key_bias(cut):
    q = lax.broadcasted_iota(jnp.int32, (PAD, PAD), 0)
    k = lax.broadcasted_iota(jnp.int32, (PAD, PAD), 1)
    hidden = k >= 72
    if cut is not None:
        hidden = hidden | (cut & ((q >= 36) != (k >= 36)))
    one = jnp.where(hidden, jnp.float32(-1e30), jnp.float32(0.0))
    return jnp.concatenate([one] * 4, axis=0)


def attend_window(qkv, ctx, row, bias, width):
    lane = lax.broadcasted_iota(jnp.int32, (PAD, 256), 1) // 64
    low = lax.broadcasted_iota(jnp.int32, (PAD, 128), 1) < 64
    rows = pl.ds(row, PAD)
    for quad in range(width // 256):
        at = quad * 256
        q = qkv[rows, at : at + 256]
        k = qkv[rows, width + at : width + at + 256]
        v = qkv[rows, 2 * width + at : 2 * width + at + 256]
        q4 = jnp.concatenate([q * (lane == h).astype(BF16) for h in range(4)], axis=0)
        s = lax.dot_general(q4, k, (((1,), (1,)), ((), ())), preferred_element_type=F32) + bias
        p = jnp.exp2((s - jnp.max(s, axis=-1, keepdims=True)) * SCALE)
        total = jnp.sum(p, axis=-1, keepdims=True)
        o = mm(p.astype(BF16), v) * (1.0 / total)
        left = jnp.where(low, o[0:PAD, 0:128], o[PAD : 2 * PAD, 0:128])
        right = jnp.where(low, o[2 * PAD : 3 * PAD, 128:256], o[3 * PAD :, 128:256])
        ctx[rows, at : at + 128] = left.astype(BF16)
        ctx[rows, at + 128 : at + 256] = right.astype(BF16)


def kernel(remote, *refs):
    r = dict(zip(NAMES, refs, strict=True))
    x, xe, c, fine, fe, fc, s, z, w, qkv, ctx, hid, xw, qkv1, ctx1, xn2, acc = (
        r[n] for n in BUFFERS
    )

    lat, lon = lax.axis_index("lat"), lax.axis_index("lon")
    lats, lons = lax.axis_size("lat"), lax.axis_size("lon")
    zs = max(lons // 4, 1)
    y_lo, core = lat % 2, lon % 2
    zi, y_hi = (lon // 2) % zs, lon // (2 * zs)
    north, south = (lat + lats - 1) % lats, (lat + 1) % lats
    west, east = (lon + lons - 1) % lons, (lon + 1) % lons

    def at_z(k):
        return y_hi * (2 * zs) + ((zi + k + zs) % zs) * 2 + core

    other = (lat - y_lo + (1 - y_lo), (1 - y_hi) * (2 * zs) + zi * 2 + core)
    next_x, last_x = ((lat + 2) % lats, lon), ((lat + lats - 2) % lats, lon)
    twin = (lat, lon - core + (1 - core))
    up_z, down_z = (lat, at_z(1)), (lat, at_z(-1))

    def load(i, src, dst):
        copy = pltpu.make_async_copy(src, dst, r["lsem"].at[i])
        copy.start()
        return copy

    shard = pl.ds(pl.multiple_of(lon * 32, 32), 32)
    load_x = load(0, r["tokens"], x.at[pl.ds(0, 1152)])
    load_ci = load(1, r["ci"], w.at[shard, pl.ds(0, 3072)])
    load_co = load(2, r["co"], w.at[shard, pl.ds(3072, 1024)])
    loads = {}

    def fetch(*which):
        for n in which:
            loads[n] = load(3 + ORDER.index(n), r[n], r["v" + n])

    fetch("east1", "own1", "wi")

    def need(*which):
        for n in which:
            loads.pop(n).wait()

    if remote:
        barrier = pltpu.get_barrier_semaphore()
        partners = [
            (north, lon), (south, lon), (lat, west), (lat, east), (north, west), (south, east),
            up_z, down_z, other, next_x, last_x, twin,
        ]
        for partner in partners:
            pl.semaphore_signal(barrier, inc=1, device_id=partner, device_id_type=MESH)

    def send(pair, i, src, dst, device):
        copy = pltpu.make_async_remote_copy(
            src_ref=src, dst_ref=dst, send_sem=r[pair + "send"].at[i],
            recv_sem=r[pair + "recv"].at[i], device_id=device, device_id_type=MESH,
        )
        if remote:
            copy.start()
        return copy

    sent = []

    def halo(i, src, dst, device):
        copy = send("h", i, src, dst, device)
        sent.append(copy)
        return copy

    def arrive(*copies):
        if remote:
            for copy in copies:
                copy.wait_recv()

    seq = [0, -1, 1, -2, 2, -3, 3, 4]
    pick = (lat // 2) % 2

    def rows_of(half, k, start=0, count=32):
        first = (half * (2 * zs) + ((zi + k + zs) % zs) * 2 + core) * 32 + start
        return w.at[pl.ds(pl.multiple_of(first, 16), count)]

    got = {}

    def push(key, i, ref, device):
        got[key] = send("g", i, ref, ref, device)
        sent.append(got[key])

    def half(k, part):
        return rows_of(y_hi, k, 16 * ((pick + part) % 2), 16)

    def push_up(step, part):
        push(("up", step, part), 2 * step + part, half(-step, part), up_z)

    def push_down(step, part):
        i = 7 + (6 if step == 3 else 2 * step + part)
        push(("down", step, part), i, half(step, part), down_z)

    def push_other(n):
        push(("other", n), 14 + n, half(seq[n], 0), other)

    def push_x(n):
        arrive(got["other", n])
        mine = rows_of(1 - y_hi, seq[n], 16 * pick, 16)
        push(("left", n), 22 + 2 * n, mine.at[:, pl.ds(0, 2048)], last_x)
        push(("right", n), 23 + 2 * n, mine.at[:, pl.ds(2048, 2048)], next_x)

    def push_near(n):
        push(("near", n), 38 + n, rows_of(y_hi, seq[n]), twin)

    def push_far(n):
        arrive(got["left", n], got["right", n])
        push(("far", n), 46 + n, rows_of(1 - y_hi, seq[n]), twin)

    def gather_round(j):
        if j == 0:
            load_ci.wait()
            load_co.wait()
            for part in range(2):
                push_up(0, part)
                push_down(0, part)
            push_other(0)
            push_near(0)
        elif j <= 6:
            step, part = (j - 1) // 2, (j - 1) % 2
            arrive(got["up", step, part])
            if step < 2 or part == 0:
                push_up(step + 1, part)
            arrive(got["down", step, part])
            if step < 2 or part == 1:
                push_down(step + 1, part)
            for n in (2 * step + 1, 2 * step + 2):
                push_near(n) if part else push_other(n)
        elif j == 7:
            arrive(got["up", 3, 0])
            push_other(7)
            arrive(got["down", 3, 1])
            push_near(7)
        if 1 <= j <= 8:
            push_x(j - 1)
        if 2 <= j <= 9:
            push_far(j - 2)
        if j == 10:
            arrive(*(got["near", n] for n in range(8)))
        if j == 11:
            arrive(*(got["far", n] for n in range(8)))

    ticks = []

    def tick():
        for j in PLAN.get(len(ticks), ()):
            gather_round(j)
        ticks.append(0)

    plain = key_bias(None)
    seam = key_bias(lat == lats - 1)
    load_x.wait()
    need("east1")
    for g in range(3):
        c[48 * g : 48 * g + 48] = mm(
            r["veast1"][...], x[384 * g : 384 * g + 384]
        ).astype(BF16)
    if remote:
        pl.semaphore_wait(barrier, len(partners))
    row_in = halo(0, x.at[pl.ds(0, 144)], x.at[pl.ds(1152, 144)], (north, lon))
    col_in = halo(1, c, xe.at[pl.ds(0, 144)], (lat, west))
    end_in = halo(2, c.at[pl.ds(0, 32)], xe.at[pl.ds(144, 32)], (north, west))
    gather_round(0)
    fetch("halo1", "wo", "we", "wr")

    fine[16:20, 48:80] = jnp.zeros((4, 32, 512), BF16)

    need("own1", "wi")
    for b in range(3):
        at = slice(320 * b, 320 * b + 240)
        wx = mm(r["vown1"][0:240], x[(6 * b + 3) * 48 : (6 * b + 9) * 48])
        xw[at] = wx.astype(BF16)
        qkv1[at] = mm(norm(wx, r["g1"][...]), r["vwi"][...]).astype(BF16)
        for k in range(3):
            attend_window(qkv1, ctx1, 320 * b + k * PAD, plain, 512)
        tick()

    fetch("east2", "join", "wm", "leave", "stay", "enter")
    arrive(row_in, col_in, end_in)
    need("halo1")
    edges = []
    for b in range(4):
        part = slice(240, 320) if b < 3 else slice(0, 320)
        wx = mm(r["vown1"][part], x[(6 * b + 3) * 48 : (6 * b + 9) * 48])
        wx = wx + mm(r["vhalo1"][b, part], xe[32 * b + 16 : 32 * b + 80])
        xw[320 * b + part.start : 320 * b + 320] = wx.astype(BF16)
        edges.append(norm(wx, r["g1"][...]))
    edges = jnp.concatenate(edges, axis=0)
    for j in range(3):
        some = slice(512 * j, 512 * j + 512)
        made = mm(edges, r["vwi"][:, some]).astype(BF16)
        for b in range(3):
            qkv1[320 * b + 240 : 320 * b + 320, some] = made[80 * b : 80 * b + 80]
        qkv1[960:1280, some] = made[240:560]
    tick()
    for b in range(3):
        attend_window(qkv1, ctx1, 320 * b + 240, plain, 512)
    tick()
    for k in range(4):
        attend_window(qkv1, ctx1, 960 + k * PAD, seam, 512)
    tick()
    need("wo", "we", "wr")

    def feed(slots):
        parts = []
        for start, count in slots:
            at = slice(PAD * start, PAD * (start + count))
            first = xw[at].astype(F32) + mm(ctx1[at], r["vwo"][...])
            parts += [first[PAD * k : PAD * k + 72] for k in range(count)]
        f = jnp.concatenate(parts, axis=0).astype(BF16).astype(F32)
        fn = norm(f, r["g2"][...])
        size = f.shape[0]
        for j in range(4):
            some = slice(512 * j, 512 * j + 512)
            hid[0:size, some] = gelu(mm(fn, r["vwe"][:, some])).astype(BF16)
            tick()
        total = f + mm(hid[0:size], r["vwr"][...])
        blank = jnp.zeros((PAD - 72, 512), F32)
        at = 0
        for start, count in slots:
            for k in range(count):
                whole = jnp.concatenate([total[at : at + 72], blank], axis=0)
                fine[start + k] = whole.astype(BF16)
                at += 72
        tick()

    feed([(0, 4), (4, 1), (8, 1), (12, 1)])
    need("east2")
    west_edge = jnp.concatenate([fine[4 * b] for b in range(4)], axis=0)
    fc[...] = mm(r["veast2"][...], west_edge).astype(BF16)
    row_in = halo(
        3, fine.at[pl.ds(0, 4), pl.ds(0, 48)], fine.at[pl.ds(16, 4), pl.ds(0, 48)], (north, lon)
    )
    col_in = halo(4, fc, fe.at[pl.ds(0, 144)], (lat, west))
    end_in = halo(5, fc.at[pl.ds(0, 32)], fe.at[pl.ds(144, 32)], (north, west))
    feed([(5, 3), (9, 3), (13, 3)])

    need("join", "wm")
    arrive(row_in, col_in, end_in)
    blocks = []
    for a in range(2):
        bands = fine[8 * a : 8 * a + 12].reshape(960, 512)
        start = (16, 80)[a]
        blocks.append(
            mm(r["vjoin"][a, :, 0:960], bands)
            + mm(r["vjoin"][a, :, 960:1056], fe[start : start + 96])
        )
    members = [
        jnp.concatenate([blocks[a][160 * k : 160 * k + 160] for a in range(2)], axis=0)
        for k in range(4)
    ]
    tick()
    mean = sum(jnp.sum(v, -1, keepdims=True) for v in members) * (1 / 2048)
    members = [v - mean for v in members]
    factor = lax.rsqrt(
        sum(jnp.sum(v * v, -1, keepdims=True) for v in members) * (1 / 2048) + EPS
    )
    joined = jnp.concatenate(
        [
            (v * factor * r["gm"][:, 512 * k : 512 * k + 512]).astype(BF16)
            for k, v in enumerate(members)
        ],
        axis=1,
    )
    wx = mm(joined, r["vwm"][...]).astype(BF16).astype(F32)
    tick()

    need("leave", "stay", "enter")
    xn = norm(wx, r["gc"][...])
    xn2[0] = xn[:, 0:512]
    xn2[1] = xn[:, 512:1024]
    depth = w.shape[0] // 2
    near = pl.ds(pl.multiple_of(y_hi * depth, depth), depth)
    far = pl.ds(pl.multiple_of((1 - y_hi) * depth, depth), depth)
    for j in range(6):
        some = slice(512 * j, 512 * j + 512)
        acc[:, some] = mm(xn2[y_hi], w[near, some])
        tick()
    for j in range(6):
        some = slice(512 * j, 512 * j + 512)
        qkv[:, some] = (acc[:, some] + mm(xn2[1 - y_hi], w[far, some])).astype(BF16)
    for k in (3, 2, 1):
        attend_window(qkv, ctx, k * PAD, seam if k >= 2 else plain, 1024)
    y_edge = (wx[PAD:] + mm(ctx[PAD:320], w[:, 3072:4096])).astype(BF16)
    s[...] = mm(r["vleave"][...], y_edge).astype(BF16)
    row_back = halo(6, s.at[pl.ds(0, 64)], z.at[pl.ds(0, 64)], (south, lon))
    col_back = halo(7, s.at[pl.ds(64, 64)], z.at[pl.ds(64, 64)], (lat, east))
    end_back = halo(8, s.at[pl.ds(128, 32)], z.at[pl.ds(128, 32)], (south, east))
    attend_window(qkv, ctx, 0, plain, 1024)
    y_rest = (wx[0:PAD] + mm(ctx[0:PAD], w[:, 3072:4096])).astype(BF16)
    kept = mm(r["vstay"][...], jnp.concatenate([y_rest, y_edge], axis=0))
    arrive(row_back, col_back, end_back)
    r["out"][...] = (kept + mm(r["venter"][...], z[...])).astype(BF16)
    if remote:
        for copy in sent:
            copy.wait_send()


PLAN = {
    2: (1,), 4: (2,), 6: (3,), 9: (4,), 11: (5,), 14: (6,), 15: (7,), 17: (8, 10), 20: (9,),
    23: (11,),
}


def per_device(remote, *args):
    tokens, g1, wi, wo, g2, we, wr, gm, wm, gc, ci, co = args
    consts = [jnp.asarray(t) for t in tables()]
    operands = [
        tokens.reshape(1152, 512), g1.reshape(1, -1), wi, wo, g2.reshape(1, -1), we, wr,
        gm.reshape(1, -1), wm, gc.reshape(1, -1), ci, co, *consts,
    ]
    hbm = pl.BlockSpec(memory_space=pl.ANY)
    vmem = pl.BlockSpec(memory_space=pltpu.VMEM)
    small = (1, 4, 7, 9)
    held = [wi, wo, we, wr, wm, *consts]
    scratch = [
        pltpu.VMEM((1296, 512), BF16),
        pltpu.VMEM((176, 512), BF16),
        pltpu.VMEM((144, 512), BF16),
        pltpu.VMEM((20, PAD, 512), BF16),
        pltpu.VMEM((176, 512), BF16),
        pltpu.VMEM((144, 512), BF16),
        pltpu.VMEM((160, 1024), BF16),
        pltpu.VMEM((160, 1024), BF16),
        pltpu.VMEM((1024, 4096), BF16),
        pltpu.VMEM((320, 3072), BF16),
        pltpu.VMEM((320, 1024), BF16),
        pltpu.VMEM((648, 2048), BF16),
        pltpu.VMEM((1280, 512), BF16),
        pltpu.VMEM((1280, 1536), BF16),
        pltpu.VMEM((1280, 512), BF16),
        pltpu.VMEM((2, 320, 512), BF16),
        pltpu.VMEM((320, 3072), F32),
        *(pltpu.VMEM(a.shape, BF16) for a in held),
        pltpu.SemaphoreType.DMA((3 + len(ORDER),)),
        pltpu.SemaphoreType.DMA((10,)),
        pltpu.SemaphoreType.DMA((10,)),
        pltpu.SemaphoreType.DMA((54,)),
        pltpu.SemaphoreType.DMA((54,)),
    ]
    params = dict(collective_id=0, has_side_effects=True) if remote else {}
    out = pl.pallas_call(
        functools.partial(kernel, remote),
        out_shape=jax.ShapeDtypeStruct((288, 1024), BF16),
        in_specs=[vmem if i in small else hbm for i in range(len(operands))],
        out_specs=vmem,
        scratch_shapes=scratch,
        compiler_params=pltpu.CompilerParams(vmem_limit_bytes=60 * 1024 * 1024, **params),
        name="encoder",
    )(*operands)
    return out.reshape(12, 24, 1024)


def solution(mesh, remote=True):
    return jax.shard_map(
        functools.partial(per_device, remote),
        mesh=mesh,
        in_specs=(P("lat", "lon", None), *[P()] * 9, P("lon", None), P("lon", None)),
        out_specs=P("lat", "lon", None),
        check_vma=False,
    )
```
